256 devices in a mesh: ao: 16 (over x, y_hi, core), aux: 16 (over y_lo, z).
Axes of the slice: x: 4, y: 4 (y_hi: 2, y_lo: 2; y = y_hi * 2 + y_lo), z: 8, core: 2. Of those that a mesh axis runs over, the one named last changes fastest.
Arguments:
- orbital_factors: float32 [32, 500, 10240], P('aux', None, 'ao'), may hold values from -1.75 to 1.75
- plan: int32 [2, 16], replicated, may hold values from 0 to 15, as said below
Outputs:
- exchange_tiles: float32 [2, 10240, 640], P(None, ('ao', 'aux'))
The draws below stay inside these ranges and needn't reach their ends.
Inputs may be any that keep to these rules, and one draw needn't show every extreme that they name: `plan`: in round r every block a has the partner a XOR s_r, with one nonzero s_r for each round and different s_r in different rounds.
All inputs are finite; a program needn't handle non-finite values.
Results may differ from the reference program's by a relative error of at most 0.0003.
Values sent between devices are 32-bit elements; how exact they have to be, the bound alone decides.
No kernel may reach another device: no remote copies, remote signals or barrier semaphores. Data moves between devices by JAX's collectives and lax.ppermute only.
A program may use at most 64 MiB of HBM per device.

```python
import jax
import jax.numpy as jnp
from jax import lax

BLK = 640
OCC = 500
Q_DEV = 2
ROUNDS = 2
NAO = 10240
QAUX = 32
N_AO = 16
N_AUX = 16


def draw_plan(key, part):
    key = jax.random.fold_in(key, 7)
    masks = jax.random.permutation(key, N_AO - 1).astype(jnp.int32) + 1
    chosen = masks[:ROUNDS]
    blocks = jnp.arange(N_AO, dtype=jnp.int32)
    return jnp.bitwise_xor(blocks[None, :], chosen[:, None]).astype(jnp.int32)


def strengthened(result, own_key, source, target, shards_of, factor):
    owner, partner = [(jnp.arange(result.shape[position]) // (result.shape[position] // shards_of)).reshape([-1 if axis == position else 1 for axis in range(result.ndim)]) for position in (source, target)]
    chosen = jax.random.permutation(own_key, shards_of)[partner]
    strong = (owner == chosen) | (owner == (partner + shards_of // 2) % shards_of)
    return jnp.where(strong, factor * result, result)


def steps_of(key, dims, pieces, least, largest):
    def one(position, parts):
        draws = jax.random.uniform(jax.random.fold_in(jax.random.fold_in(key, 6), position), (parts,), jnp.float32, least / len(pieces), largest / len(pieces))
        return jnp.repeat(jnp.exp(draws), dims[position] // parts).reshape((-1,) + (1,) * (len(dims) - position - 1))

    level = one(*pieces[0])
    for cut in pieces[1:]:
        level = level * one(*cut)
    return level


def bell_draw_with(stream_key, dims, deviation, limit, cuts, heavy, held_as=jnp.bfloat16):
    entries = deviation * jax.random.normal(stream_key, dims, jnp.float32)
    if cuts:
        entries = entries * steps_of(stream_key, dims, cuts, -0.22, 0.18)
    return jnp.clip(strengthened(entries, jax.random.fold_in(stream_key, 3), *heavy), -limit, limit).astype(held_as)


def setup_inputs(seed: int = 0) -> dict:
    key_of = jax.random.split(jax.random.key(seed), 3)
    orbital_factors = bell_draw_with(key_of[0], (QAUX, OCC, NAO), ((Q_DEV * N_AUX * OCC) ** -0.25), 1.75, ((0, 16), (2, 16)), (0, 2, 16, 2.0), jnp.float32)
    plan = draw_plan(jax.random.fold_in(key_of[2], 71), 0)
    return dict(orbital_factors=orbital_factors, plan=plan)


def reference(orbital_factors, plan):
    flat_rows = orbital_factors.reshape(QAUX * OCC, NAO)
    results = []
    for step in range(ROUNDS):
        partners = plan[step]

        def one_tile(index):
            own = lax.dynamic_slice_in_dim(flat_rows, (index * BLK).astype(jnp.int32), BLK, 1)
            other = lax.dynamic_slice_in_dim(flat_rows, (partners[index] * BLK).astype(jnp.int32), BLK, 1)
            return lax.dot_general(own, other, (((0,), (0,)), ((), ())), precision=lax.Precision.HIGHEST, preferred_element_type=jnp.float32)

        tiles = lax.map(one_tile, jnp.arange(N_AO, dtype=jnp.int32))
        results.append(tiles.reshape(NAO, BLK))
    return jnp.stack(results, 0)
```

```python
import jax
import jax.numpy as jnp
import numpy as np
from jax import lax
from jax.experimental import pallas as pl
from jax.experimental.pallas import tpu as pltpu
from jax.sharding import PartitionSpec as P

CHIPS = 8
SWAP = [(a, a ^ 1) for a in range(2 * CHIPS)]
DIMS = (((0,), (0,)), ((), ()))


def odd(value):
    return bin(value).count("1") & 1


def chip_split(low, high):
    if low >> 1 == high >> 1:
        return (low >> 1) & -(low >> 1)
    for split in range(CHIPS):
        if odd(split & (low >> 1)) == 1 ^ (low & 1) and odd(split & (high >> 1)) == 1 ^ (high & 1):
            return split


def split_table():
    table = np.zeros((2 * CHIPS, 2 * CHIPS), np.int32)
    for low in range(1, 2 * CHIPS):
        for high in range(low + 1, 2 * CHIPS):
            table[low, high] = chip_split(low, high)
    return table.reshape(-1)


def routes():
    out = []
    for high in range(1, CHIPS):
        for low in range(high):
            out.append([((d ^ (high if c else low)) * 2 + (c ^ 1), d * 2 + c) for d in range(CHIPS) for c in range(2)])
    for mask in range(1, CHIPS):
        split = mask & -mask
        out.append([((d ^ mask) * 2 + (c ^ odd(split & d)), d * 2 + c) for d in range(CHIPS) for c in range(2)])
    return out


def tile_kernel(a_ref, p_ref, o_ref, p_high, p_low):
    @pl.when(pl.program_id(0) == 0)
    def _():
        p = p_ref[...]
        high = p.astype(jnp.bfloat16)
        p_high[...] = high
        p_low[...] = (p - high.astype(jnp.float32)).astype(jnp.bfloat16)

    a = a_ref[...]
    high = a.astype(jnp.bfloat16)
    low = (a - high.astype(jnp.float32)).astype(jnp.bfloat16)
    total = None
    for left, right in ((low, p_high), (high, p_low), (high, p_high)):
        part = lax.dot_general(left, right[...], DIMS, preferred_element_type=jnp.float32)
        total = part if total is None else total + part
    o_ref[...] = total


def tile_of(block, partner):
    depth, width = block.shape
    rows = 128
    return pl.pallas_call(
        tile_kernel,
        grid=(width // rows,),
        out_shape=jax.ShapeDtypeStruct((width, width), jnp.float32),
        in_specs=[
            pl.BlockSpec((depth, rows), lambda i: (0, i)),
            pl.BlockSpec((depth, width), lambda i: (0, 0)),
        ],
        out_specs=pl.BlockSpec((rows, width), lambda i: (i, 0)),
        scratch_shapes=[pltpu.VMEM((depth, width), jnp.bfloat16)] * 2,
        compiler_params=pltpu.CompilerParams(vmem_limit_bytes=32 << 20),
    )(block, partner)


def local(orbital_factors, plan):
    parts = lax.axis_size("aux")
    own = lax.axis_index("ao")
    chip, core = own >> 1, own & 1
    low, high = jnp.min(plan[:, 0]), jnp.max(plan[:, 0])
    low_round = jnp.where(plan[0, 0] == low, 0, 1)
    low_chip, high_chip = low >> 1, high >> 1
    same = low_chip == high_chip
    split = jnp.asarray(split_table())[low * (2 * CHIPS) + high]
    side = lax.population_count(chip & split) & 1
    own_round = low_round ^ jnp.where(same, side, core ^ side)
    case = jnp.where(same, 27 + low_chip, (high_chip * (high_chip - 1) >> 1) + low_chip)
    mask = jnp.where(core == 1, high_chip, low_chip)

    width = orbital_factors.shape[2]
    rows = lax.optimization_barrier(jnp.swapaxes(orbital_factors, 0, 1).reshape(-1, width))
    sibling = lax.ppermute(rows, "ao", SWAP)
    block = lax.optimization_barrier(jnp.where((side == 1) & ~same, sibling, rows))
    partner = lax.switch(
        case, [lambda x, r=r: lax.ppermute(x, "ao", r) for r in routes()], block
    )
    tile = tile_of(block, partner)
    share = width // parts
    slabs = lax.all_to_all(tile.reshape(parts, share, width), "aux", 0, 0)
    mine = jnp.sum(slabs, 0)
    flipped = mine.T.reshape(parts, share, share)
    cross = lax.all_to_all(flipped, "aux", 0, 0)
    theirs = jnp.moveaxis(cross, 0, 1).reshape(share, width)
    for bit in range(3):
        moved = lax.ppermute(theirs, "ao", [(a, a ^ (2 << bit)) for a in range(2 * CHIPS)])
        theirs = jnp.where((mask >> bit) & 1 == 1, moved, theirs)
    sent = jnp.where(side == 1, mine, theirs)
    kept = jnp.where(side == 1, theirs, mine)
    got = lax.ppermute(sent, "ao", SWAP)
    got = jnp.where(same & (side == 1), sent, got)
    straight = own_round == side
    return jnp.stack([jnp.where(straight, kept, got), jnp.where(straight, got, kept)], 0)


def solution(mesh):
    placed = (P("aux", None, "ao"), P())
    return jax.shard_map(
        local, mesh=mesh, in_specs=placed, out_specs=P(None, ("ao", "aux"), None), check_vma=False
    )
```

```python
import jax
import jax.numpy as jnp
import numpy as np
from jax import lax
from jax.experimental import pallas as pl
from jax.experimental.pallas import tpu as pltpu
from jax.sharding import PartitionSpec as P

CHIPS = 8
SWAP = [(a, a ^ 1) for a in range(2 * CHIPS)]
CUTS = ((0, 640),)
DIMS = (((0,), (0,)), ((), ()))


def odd(value):
    return bin(value).count("1") & 1


def chip_split(low, high):
    if low >> 1 == high >> 1:
        return (low >> 1) & -(low >> 1)
    for split in range(CHIPS):
        if odd(split & (low >> 1)) == 1 ^ (low & 1) and odd(split & (high >> 1)) == 1 ^ (high & 1):
            return split


def split_table():
    table = np.zeros((2 * CHIPS, 2 * CHIPS), np.int32)
    for low in range(1, 2 * CHIPS):
        for high in range(low + 1, 2 * CHIPS):
            table[low, high] = chip_split(low, high)
    return table.reshape(-1)


def by_mask(x, mask, core):
    branches = [lambda x: x]
    for c in range(2):
        for m in range(1, CHIPS):
            route = [((d ^ m) * 2 + c, d * 2 + c) for d in range(CHIPS)]
            branches.append(lambda x, route=route: lax.ppermute(x, "ao", route))
    case = jnp.where(mask == 0, 0, mask + (CHIPS - 1) * core)
    return lax.switch(case, branches, x)


def tile_kernel(a_ref, p_ref, o_ref, p_high, p_low):
    @pl.when(pl.program_id(0) == 0)
    def _():
        p = p_ref[...]
        high = p.astype(jnp.bfloat16)
        p_high[...] = high
        p_low[...] = (p - high.astype(jnp.float32)).astype(jnp.bfloat16)

    a = a_ref[...]
    high = a.astype(jnp.bfloat16)
    low = (a - high.astype(jnp.float32)).astype(jnp.bfloat16)
    total = None
    for left, right in ((low, p_high), (high, p_low), (high, p_high)):
        part = lax.dot_general(left, right[...], DIMS, preferred_element_type=jnp.float32)
        total = part if total is None else total + part
    o_ref[...] = total


def tile_of(block, partner):
    depth, width = block.shape
    columns = partner.shape[1]
    rows = 128
    return pl.pallas_call(
        tile_kernel,
        grid=(width // rows,),
        out_shape=jax.ShapeDtypeStruct((width, columns), jnp.float32),
        in_specs=[
            pl.BlockSpec((depth, rows), lambda i: (0, i)),
            pl.BlockSpec((depth, columns), lambda i: (0, 0)),
        ],
        out_specs=pl.BlockSpec((rows, columns), lambda i: (i, 0)),
        scratch_shapes=[pltpu.VMEM((depth, columns), jnp.bfloat16)] * 2,
        compiler_params=pltpu.CompilerParams(vmem_limit_bytes=32 << 20),
    )(block, partner)


def local(orbital_factors, plan):
    parts = lax.axis_size("aux")
    own = lax.axis_index("ao")
    chip, core = own >> 1, own & 1
    low, high = jnp.min(plan[:, 0]), jnp.max(plan[:, 0])
    low_round = jnp.where(plan[0, 0] == low, 0, 1)
    low_chip, high_chip = low >> 1, high >> 1
    same = low_chip == high_chip
    split = jnp.asarray(split_table())[low * (2 * CHIPS) + high]
    side = lax.population_count(chip & split) & 1
    own_round = low_round ^ jnp.where(same, side, core ^ side)
    mask = jnp.where(core == 1, high_chip, low_chip)

    width = orbital_factors.shape[2]
    share = width // parts
    rows = lax.optimization_barrier(jnp.swapaxes(orbital_factors, 0, 1).reshape(-1, width))
    sibling = lax.ppermute(rows, "ao", SWAP)
    block = jnp.where((side == 1) & ~same, sibling, rows)
    sums = []
    for start, stop in CUTS:
        piece = jnp.where(side == 1, rows[:, start:stop], sibling[:, start:stop])
        piece = by_mask(lax.optimization_barrier(piece), mask, core)
        tile = tile_of(block, piece)
        slabs = lax.all_to_all(tile.reshape(parts, share, stop - start), "aux", 0, 0)
        sums.append(jnp.sum(slabs, 0))
    mine = jnp.concatenate(sums, 1)
    flipped = mine.T.reshape(parts, share, share)
    cross = lax.all_to_all(flipped, "aux", 0, 0)
    theirs = jnp.moveaxis(cross, 0, 1).reshape(share, width)
    theirs = by_mask(theirs, mask, core)
    sent = jnp.where(side == 1, mine, theirs)
    kept = jnp.where(side == 1, theirs, mine)
    got = lax.ppermute(sent, "ao", SWAP)
    got = jnp.where(same & (side == 1), sent, got)
    straight = own_round == side
    return jnp.stack([jnp.where(straight, kept, got), jnp.where(straight, got, kept)], 0)


def solution(mesh):
    placed = (P("aux", None, "ao"), P())
    return jax.shard_map(
        local, mesh=mesh, in_specs=placed, out_specs=P(None, ("ao", "aux"), None), check_vma=False
    )
```

```python
import jax
import jax.numpy as jnp
import numpy as np
from jax import lax
from jax.experimental import pallas as pl
from jax.experimental.pallas import tpu as pltpu
from jax.sharding import PartitionSpec as P

CHIPS = 8
SWAP = [(a, a ^ 1) for a in range(2 * CHIPS)]
RING = 8
ORDER = (0, 3, 4, 7, 1, 6, 2, 5)
ACROSS = {0: 3, 3: 0, 4: 7, 7: 4, 1: 6, 6: 1, 2: 5, 5: 2}
STREAMS = ((0, 384, ("y", 0, 1, 2)), (384, 640, (0, "y", 1, 2)))
DIMS = (((0,), (0,)), ((), ()))


def odd(value):
    return bin(value).count("1") & 1


def chip_split(low, high):
    if low >> 1 == high >> 1:
        return (low >> 1) & -(low >> 1)
    for split in range(CHIPS):
        if odd(split & (low >> 1)) == 1 ^ (low & 1) and odd(split & (high >> 1)) == 1 ^ (high & 1):
            return split


def split_table():
    table = np.zeros((2 * CHIPS, 2 * CHIPS), np.int32)
    for low in range(1, 2 * CHIPS):
        for high in range(low + 1, 2 * CHIPS):
            table[low, high] = chip_split(low, high)
    return table.reshape(-1)


def routes():
    out = []
    for high in range(1, CHIPS):
        for low in range(high):
            out.append([((d ^ (high if c else low)) * 2 + (c ^ 1), d * 2 + c) for d in range(CHIPS) for c in range(2)])
    for mask in range(1, CHIPS):
        split = mask & -mask
        out.append([((d ^ mask) * 2 + (c ^ odd(split & d)), d * 2 + c) for d in range(CHIPS) for c in range(2)])
    return out


def ring_partner(z, step):
    if step == 0:
        return z ^ 1
    if step == 1:
        return (((z + 1) ^ 1) - 1) % RING
    return ACROSS[z]


def sums_of(tile, share):
    me = lax.axis_index("aux")
    place = jnp.asarray(np.argsort(ORDER).astype(np.int32))[me % RING]
    bit_of = {"y": me // RING, 0: place >> 2, 1: (place >> 1) & 1, 2: place & 1}
    streams = []
    for start, stop, steps in STREAMS:
        slabs = tile[:, start:stop].reshape(2, RING, share, stop - start)
        slabs = jnp.stack([slabs[:, z] for z in ORDER], 1)
        streams.append((slabs.reshape(2, 2, 2, 2, share, stop - start), ["y", 0, 1, 2], steps))
    for turn in range(4):
        after = []
        for slabs, axes, steps in streams:
            step = steps[turn]
            axis, bit = axes.index(step), bit_of[step]
            if step == "y":
                route = [(k, k ^ RING) for k in range(2 * RING)]
            else:
                route = [(k, k // RING * RING + ring_partner(k % RING, step)) for k in range(2 * RING)]
            away = lax.ppermute(lax.dynamic_index_in_dim(slabs, 1 - bit, axis, False), "aux", route)
            kept = lax.dynamic_index_in_dim(slabs, bit, axis, False)
            after.append((kept + away, [a for a in axes if a != step], steps))
        streams = after
    return jnp.concatenate([slabs for slabs, _, _ in streams], 1)


def tile_kernel(a_ref, p_ref, o_ref, p_high, p_low):
    @pl.when(pl.program_id(0) == 0)
    def _():
        p = p_ref[...]
        high = p.astype(jnp.bfloat16)
        p_high[...] = high
        p_low[...] = (p - high.astype(jnp.float32)).astype(jnp.bfloat16)

    a = a_ref[...]
    high = a.astype(jnp.bfloat16)
    low = (a - high.astype(jnp.float32)).astype(jnp.bfloat16)
    total = None
    for left, right in ((low, p_high), (high, p_low), (high, p_high)):
        part = lax.dot_general(left, right[...], DIMS, preferred_element_type=jnp.float32)
        total = part if total is None else total + part
    o_ref[...] = total


def tile_of(block, partner):
    depth, width = block.shape
    rows = 128
    return pl.pallas_call(
        tile_kernel,
        grid=(width // rows,),
        out_shape=jax.ShapeDtypeStruct((width, width), jnp.float32),
        in_specs=[
            pl.BlockSpec((depth, rows), lambda i: (0, i)),
            pl.BlockSpec((depth, width), lambda i: (0, 0)),
        ],
        out_specs=pl.BlockSpec((rows, width), lambda i: (i, 0)),
        scratch_shapes=[pltpu.VMEM((depth, width), jnp.bfloat16)] * 2,
        compiler_params=pltpu.CompilerParams(vmem_limit_bytes=32 << 20),
    )(block, partner)


def local(orbital_factors, plan):
    parts = lax.axis_size("aux")
    own = lax.axis_index("ao")
    chip, core = own >> 1, own & 1
    low, high = jnp.min(plan[:, 0]), jnp.max(plan[:, 0])
    low_round = jnp.where(plan[0, 0] == low, 0, 1)
    low_chip, high_chip = low >> 1, high >> 1
    same = low_chip == high_chip
    split = jnp.asarray(split_table())[low * (2 * CHIPS) + high]
    side = lax.population_count(chip & split) & 1
    own_round = low_round ^ jnp.where(same, side, core ^ side)
    case = jnp.where(same, 27 + low_chip, (high_chip * (high_chip - 1) >> 1) + low_chip)
    mask = jnp.where(core == 1, high_chip, low_chip)

    width = orbital_factors.shape[2]
    rows = lax.optimization_barrier(jnp.swapaxes(orbital_factors, 0, 1).reshape(-1, width))
    sibling = lax.ppermute(rows, "ao", SWAP)
    block = lax.optimization_barrier(jnp.where((side == 1) & ~same, sibling, rows))
    partner = lax.switch(
        case, [lambda x, r=r: lax.ppermute(x, "ao", r) for r in routes()], block
    )
    tile = tile_of(block, partner)
    share = width // parts
    mine = sums_of(tile, share)
    flipped = mine.T.reshape(parts, share, share)
    cross = lax.all_to_all(flipped, "aux", 0, 0)
    theirs = jnp.moveaxis(cross, 0, 1).reshape(share, width)
    for bit in range(3):
        route = [(a, a ^ (2 << bit)) for a in range(2 * CHIPS)]
        taken = (mask >> bit) & 1 == 1
        theirs = lax.cond(
            ((low_chip | high_chip) >> bit) & 1 == 1,
            lambda x, taken, route=route: jnp.where(taken, lax.ppermute(x, "ao", route), x),
            lambda x, taken: x,
            theirs,
            taken,
        )
    sent = jnp.where(side == 1, mine, theirs)
    kept = jnp.where(side == 1, theirs, mine)
    got = lax.ppermute(sent, "ao", SWAP)
    got = jnp.where(same & (side == 1), sent, got)
    straight = own_round == side
    return jnp.stack([jnp.where(straight, kept, got), jnp.where(straight, got, kept)], 0)


def solution(mesh):
    placed = (P("aux", None, "ao"), P())
    return jax.shard_map(
        local, mesh=mesh, in_specs=placed, out_specs=P(None, ("ao", "aux"), None), check_vma=False
    )
```

```python
import jax
import jax.numpy as jnp
import numpy as np
from jax import lax
from jax.experimental import pallas as pl
from jax.experimental.pallas import tpu as pltpu
from jax.sharding import PartitionSpec as P

CHIPS = 8
SWAP = [(a, a ^ 1) for a in range(2 * CHIPS)]
RING = 8
ORDER = (0, 3, 4, 7, 1, 6, 2, 5)
ACROSS = {0: 3, 3: 0, 4: 7, 7: 4, 1: 6, 6: 1, 2: 5, 5: 2}
STREAMS = ((0, 384, ("y", 0, 1, 2)), (384, 640, (0, "y", 1, 2)))
DIMS = (((0,), (0,)), ((), ()))


def odd(value):
    return bin(value).count("1") & 1


def chip_split(low, high):
    if low >> 1 == high >> 1:
        return (low >> 1) & -(low >> 1)
    for split in range(CHIPS):
        if odd(split & (low >> 1)) == 1 ^ (low & 1) and odd(split & (high >> 1)) == 1 ^ (high & 1):
            return split


def split_table():
    table = np.zeros((2 * CHIPS, 2 * CHIPS), np.int32)
    for low in range(1, 2 * CHIPS):
        for high in range(low + 1, 2 * CHIPS):
            table[low, high] = chip_split(low, high)
    return table.reshape(-1)


def by_mask(x, mask, core):
    branches = [lambda x: x]
    for c in range(2):
        for m in range(1, CHIPS):
            route = [((d ^ m) * 2 + c, d * 2 + c) for d in range(CHIPS)]
            branches.append(lambda x, route=route: lax.ppermute(x, "ao", route))
    case = jnp.where(mask == 0, 0, mask + (CHIPS - 1) * core)
    return lax.switch(case, branches, x)


def ring_partner(z, step):
    if step == 0:
        return z ^ 1
    if step == 1:
        return (((z + 1) ^ 1) - 1) % RING
    return ACROSS[z]


def sums_of(tile, share):
    me = lax.axis_index("aux")
    place = jnp.asarray(np.argsort(ORDER).astype(np.int32))[me % RING]
    bit_of = {"y": me // RING, 0: place >> 2, 1: (place >> 1) & 1, 2: place & 1}
    streams = []
    for start, stop, steps in STREAMS:
        slabs = tile[:, start:stop].reshape(2, RING, share, stop - start)
        slabs = jnp.stack([slabs[:, z] for z in ORDER], 1)
        streams.append((slabs.reshape(2, 2, 2, 2, share, stop - start), ["y", 0, 1, 2], steps))
    for turn in range(4):
        after = []
        for slabs, axes, steps in streams:
            step = steps[turn]
            axis, bit = axes.index(step), bit_of[step]
            if step == "y":
                route = [(k, k ^ RING) for k in range(2 * RING)]
            else:
                route = [(k, k // RING * RING + ring_partner(k % RING, step)) for k in range(2 * RING)]
            away = lax.ppermute(lax.dynamic_index_in_dim(slabs, 1 - bit, axis, False), "aux", route)
            kept = lax.dynamic_index_in_dim(slabs, bit, axis, False)
            after.append((kept + away, [a for a in axes if a != step], steps))
        streams = after
    return jnp.concatenate([slabs for slabs, _, _ in streams], 1)


def tile_kernel(a_ref, p_ref, o_ref, p_high, p_low):
    @pl.when(pl.program_id(0) == 0)
    def _():
        p = p_ref[...]
        high = p.astype(jnp.bfloat16)
        p_high[...] = high
        p_low[...] = (p - high.astype(jnp.float32)).astype(jnp.bfloat16)

    a = a_ref[...]
    high = a.astype(jnp.bfloat16)
    low = (a - high.astype(jnp.float32)).astype(jnp.bfloat16)
    total = None
    for left, right in ((low, p_high), (high, p_low), (high, p_high)):
        part = lax.dot_general(left, right[...], DIMS, preferred_element_type=jnp.float32)
        total = part if total is None else total + part
    o_ref[...] = total


def tile_of(block, partner):
    depth, width = block.shape
    columns = partner.shape[1]
    rows = 128
    return pl.pallas_call(
        tile_kernel,
        grid=(width // rows,),
        out_shape=jax.ShapeDtypeStruct((width, columns), jnp.float32),
        in_specs=[
            pl.BlockSpec((depth, rows), lambda i: (0, i)),
            pl.BlockSpec((depth, columns), lambda i: (0, 0)),
        ],
        out_specs=pl.BlockSpec((rows, columns), lambda i: (i, 0)),
        scratch_shapes=[pltpu.VMEM((depth, columns), jnp.bfloat16)] * 2,
        compiler_params=pltpu.CompilerParams(vmem_limit_bytes=32 << 20),
    )(block, partner)


def local(orbital_factors, plan):
    parts = lax.axis_size("aux")
    own = lax.axis_index("ao")
    chip, core = own >> 1, own & 1
    low, high = jnp.min(plan[:, 0]), jnp.max(plan[:, 0])
    low_round = jnp.where(plan[0, 0] == low, 0, 1)
    low_chip, high_chip = low >> 1, high >> 1
    same = low_chip == high_chip
    split = jnp.asarray(split_table())[low * (2 * CHIPS) + high]
    side = lax.population_count(chip & split) & 1
    own_round = low_round ^ jnp.where(same, side, core ^ side)
    mask = jnp.where(core == 1, high_chip, low_chip)

    width = orbital_factors.shape[2]
    share = width // parts
    rows = lax.optimization_barrier(jnp.swapaxes(orbital_factors, 0, 1).reshape(-1, width))
    sibling = lax.ppermute(rows, "ao", SWAP)
    block = jnp.where((side == 1) & ~same, sibling, rows)
    piece = jnp.where(side == 1, rows, sibling)
    partner = by_mask(lax.optimization_barrier(piece), mask, core)
    mine = sums_of(tile_of(block, partner), share)
    flipped = mine.T.reshape(parts, share, share)
    cross = lax.all_to_all(flipped, "aux", 0, 0)
    theirs = jnp.moveaxis(cross, 0, 1).reshape(share, width)
    theirs = by_mask(theirs, mask, core)
    sent = jnp.where(side == 1, mine, theirs)
    kept = jnp.where(side == 1, theirs, mine)
    got = lax.ppermute(sent, "ao", SWAP)
    got = jnp.where(same & (side == 1), sent, got)
    straight = own_round == side
    return jnp.stack([jnp.where(straight, kept, got), jnp.where(straight, got, kept)], 0)


def solution(mesh):
    placed = (P("aux", None, "ao"), P())
    return jax.shard_map(
        local, mesh=mesh, in_specs=placed, out_specs=P(None, ("ao", "aux"), None), check_vma=False
    )
```

```python
import jax
import jax.numpy as jnp
import numpy as np
from jax import lax
from jax.experimental import pallas as pl
from jax.experimental.pallas import tpu as pltpu
from jax.sharding import PartitionSpec as P

CHIPS = 8
SWAP = [(a, a ^ 1) for a in range(2 * CHIPS)]
RING = 8
ORDER = (0, 3, 4, 7, 1, 6, 2, 5)
ACROSS = {0: 3, 3: 0, 4: 7, 7: 4, 1: 6, 6: 1, 2: 5, 5: 2}
STREAMS = ((0, 384, 0, ("y", 0, 1, 2)), (384, 640, 1, (0, "y", 1, 2)))
DIMS = (((0,), (0,)), ((), ()))


def odd(value):
    return bin(value).count("1") & 1


def chip_split(low, high):
    if low >> 1 == high >> 1:
        return (low >> 1) & -(low >> 1)
    for split in range(CHIPS):
        if odd(split & (low >> 1)) == 1 ^ (low & 1) and odd(split & (high >> 1)) == 1 ^ (high & 1):
            return split


def split_table():
    table = np.zeros((2 * CHIPS, 2 * CHIPS), np.int32)
    for low in range(1, 2 * CHIPS):
        for high in range(low + 1, 2 * CHIPS):
            table[low, high] = chip_split(low, high)
    return table.reshape(-1)


def routes():
    out = []
    for high in range(1, CHIPS):
        for low in range(high):
            out.append([((d ^ (high if c else low)) * 2 + (c ^ 1), d * 2 + c) for d in range(CHIPS) for c in range(2)])
    for mask in range(1, CHIPS):
        split = mask & -mask
        out.append([((d ^ mask) * 2 + (c ^ odd(split & d)), d * 2 + c) for d in range(CHIPS) for c in range(2)])
    return out


def turned_partner(z, step, turn):
    return (ring_partner((z + turn) % RING, step) - turn) % RING


def ring_partner(z, step):
    if step == 0:
        return z ^ 1
    if step == 1:
        return (((z + 1) ^ 1) - 1) % RING
    return ACROSS[z]


def sums_of(tile, share):
    me = lax.axis_index("aux")
    streams = []
    for start, stop, shift, steps in STREAMS:
        place = jnp.asarray(np.argsort(ORDER).astype(np.int32))[(me + shift) % RING]
        bit_of = {"y": me // RING, 0: place >> 2, 1: (place >> 1) & 1, 2: place & 1}
        slabs = tile[:, start:stop].reshape(2, RING, share, stop - start)
        slabs = jnp.stack([slabs[:, (z - shift) % RING] for z in ORDER], 1)
        streams.append((slabs.reshape(2, 2, 2, 2, share, stop - start), ["y", 0, 1, 2], steps, shift, bit_of))
    for turn in range(4):
        after = []
        for slabs, axes, steps, shift, bit_of in streams:
            step = steps[turn]
            axis, bit = axes.index(step), bit_of[step]
            if step == "y":
                route = [(k, k ^ RING) for k in range(2 * RING)]
            else:
                route = [(k, k // RING * RING + turned_partner(k % RING, step, shift)) for k in range(2 * RING)]
            away = lax.ppermute(lax.dynamic_index_in_dim(slabs, 1 - bit, axis, False), "aux", route)
            kept = lax.dynamic_index_in_dim(slabs, bit, axis, False)
            after.append((kept + away, [a for a in axes if a != step], steps, shift, bit_of))
        streams = after
    return jnp.concatenate([stream[0] for stream in streams], 1)


def tile_kernel(a_ref, p_ref, o_ref, p_high, p_low):
    @pl.when(pl.program_id(0) == 0)
    def _():
        p = p_ref[...]
        high = p.astype(jnp.bfloat16)
        p_high[...] = high
        p_low[...] = (p - high.astype(jnp.float32)).astype(jnp.bfloat16)

    a = a_ref[...]
    high = a.astype(jnp.bfloat16)
    low = (a - high.astype(jnp.float32)).astype(jnp.bfloat16)
    total = None
    for left, right in ((low, p_high), (high, p_low), (high, p_high)):
        part = lax.dot_general(left, right[...], DIMS, preferred_element_type=jnp.float32)
        total = part if total is None else total + part
    o_ref[...] = total


def tile_of(block, partner):
    depth, width = block.shape
    rows = 128
    return pl.pallas_call(
        tile_kernel,
        grid=(width // rows,),
        out_shape=jax.ShapeDtypeStruct((width, width), jnp.float32),
        in_specs=[
            pl.BlockSpec((depth, rows), lambda i: (0, i)),
            pl.BlockSpec((depth, width), lambda i: (0, 0)),
        ],
        out_specs=pl.BlockSpec((rows, width), lambda i: (i, 0)),
        scratch_shapes=[pltpu.VMEM((depth, width), jnp.bfloat16)] * 2,
        compiler_params=pltpu.CompilerParams(vmem_limit_bytes=32 << 20),
    )(block, partner)


def local(orbital_factors, plan):
    parts = lax.axis_size("aux")
    own = lax.axis_index("ao")
    chip, core = own >> 1, own & 1
    low, high = jnp.min(plan[:, 0]), jnp.max(plan[:, 0])
    low_round = jnp.where(plan[0, 0] == low, 0, 1)
    low_chip, high_chip = low >> 1, high >> 1
    same = low_chip == high_chip
    split = jnp.asarray(split_table())[low * (2 * CHIPS) + high]
    side = lax.population_count(chip & split) & 1
    own_round = low_round ^ jnp.where(same, side, core ^ side)
    case = jnp.where(same, 27 + low_chip, (high_chip * (high_chip - 1) >> 1) + low_chip)
    mask = jnp.where(core == 1, high_chip, low_chip)

    width = orbital_factors.shape[2]
    rows = lax.optimization_barrier(jnp.swapaxes(orbital_factors, 0, 1).reshape(-1, width))
    sibling = lax.ppermute(rows, "ao", SWAP)
    block = lax.optimization_barrier(jnp.where((side == 1) & ~same, sibling, rows))
    partner = lax.switch(
        case, [lambda x, r=r: lax.ppermute(x, "ao", r) for r in routes()], block
    )
    tile = tile_of(block, partner)
    share = width // parts
    mine = sums_of(tile, share)
    flipped = mine.T.reshape(parts, share, share)
    cross = lax.all_to_all(flipped, "aux", 0, 0)
    theirs = jnp.moveaxis(cross, 0, 1).reshape(share, width)
    for bit in range(3):
        route = [(a, a ^ (2 << bit)) for a in range(2 * CHIPS)]
        taken = (mask >> bit) & 1 == 1
        theirs = lax.cond(
            ((low_chip | high_chip) >> bit) & 1 == 1,
            lambda x, taken, route=route: jnp.where(taken, lax.ppermute(x, "ao", route), x),
            lambda x, taken: x,
            theirs,
            taken,
        )
    sent = jnp.where(side == 1, mine, theirs)
    kept = jnp.where(side == 1, theirs, mine)
    got = lax.ppermute(sent, "ao", SWAP)
    got = jnp.where(same & (side == 1), sent, got)
    straight = own_round == side
    return jnp.stack([jnp.where(straight, kept, got), jnp.where(straight, got, kept)], 0)


def solution(mesh):
    placed = (P("aux", None, "ao"), P())
    return jax.shard_map(
        local, mesh=mesh, in_specs=placed, out_specs=P(None, ("ao", "aux"), None), check_vma=False
    )
```
